512 devices in a mesh: ens: 16 (over x_hi, y, core), space: 32 (over x_lo, z).
Axes of the slice: x: 4 (x_hi: 2, x_lo: 2; x = x_hi * 2 + x_lo), y: 4, z: 16, core: 2. Of those that a mesh axis runs over, the one named last changes fastest.
Arguments:
- ensemble: bfloat16 [128, 2, 1024, 512], P('ens', None, 'space'), may hold values from -6 to 6
- control: float32 [128, 2, 1024, 512], P('ens', None, 'space'), may hold values from -6 to 6
- spectrum: float32 [2, 512, 1024], P(None, 'space'), may hold values from 0.1 to 2
- row_scale: float32 [2, 1024], P(None, 'space'), may hold values from 0.5 to 2
- precision: float32 [2, 1024, 512], P(None, 'space'), may hold values from 0.5 to 8
- innovation: float32 [2, 1024, 512], P(None, 'space'), may hold values from -6 to 6
Outputs:
- gradient: float32 [128, 2, 1024, 512], P('ens', None, 'space')
The draws below stay inside these ranges and needn't reach their ends.
All inputs are finite; a program needn't handle non-finite values.
Results may differ from the reference program's by a relative error of at most 0.0003.
Values sent between devices are 32-bit elements; how exact they have to be, the bound alone decides.
A program may use at most 64 MiB of HBM per device.

```python
import math
import jax
import jax.numpy as jnp
from jax import lax

LEV = 2
NY = 512
MEMBERS = 128
NX = 1024


def level_of(rng, shape, shards, smallest, top_value):
    gain = 1.0
    for dim, parts in shards:
        steps = jax.random.uniform(jax.random.fold_in(jax.random.fold_in(rng, 6), dim), (parts,), jnp.float32, smallest / len(shards), top_value / len(shards))
        gain = gain * jnp.repeat(jnp.exp(steps), shape[dim] // parts).reshape((-1,) + (1,) * (len(shape) - 1 - dim))
    return gain


def gaussian(own_key, extent, deviation, most, pieces=(), kind=jnp.bfloat16):
    factor_of = level_of(own_key, extent, pieces, -0.22, 0.18) if pieces else 1.0
    array = jax.random.normal(own_key, extent, jnp.float32) * deviation * factor_of
    return jnp.minimum(jnp.maximum(array, -most), most).astype(kind)


def setup_inputs(seed: int = 0) -> dict:
    arg_keys = jax.random.split(jax.random.key(seed), 7)
    ensemble = gaussian(arg_keys[0], (MEMBERS, LEV, NX, NY), 1.0, 6.0, ((0, 16), (2, 32)))
    control = gaussian(arg_keys[1], (MEMBERS, LEV, NX, NY), 1.0, 6.0, ((0, 16), (2, 32)), jnp.float32)
    spectrum = jnp.clip(jnp.exp(math.log(2.0) - 2.9957323 * jax.random.uniform(arg_keys[2], (LEV, NY, NX), jnp.float32) ** level_of(arg_keys[2], (LEV, NY, NX), ((1, 32),), -0.2, 0.2)), 0.1, 2.0)
    row_scale = jnp.clip(jnp.exp(math.log(2.0) - 1.3862944 * jax.random.uniform(arg_keys[3], (LEV, NX), jnp.float32) ** level_of(arg_keys[3], (LEV, NX), ((1, 32),), -0.2, 0.2)), 0.5, 2.0)
    precision = jnp.clip(jnp.exp(math.log(8.0) - 2.7725887 * jax.random.uniform(arg_keys[4], (LEV, NX, NY), jnp.float32) ** level_of(arg_keys[4], (LEV, NX, NY), ((1, 32),), -0.2, 0.2)), 0.5, 8.0)
    innovation = gaussian(arg_keys[5], (LEV, NX, NY), 1.0, 6.0, ((1, 32),), jnp.float32)
    return {"ensemble": ensemble, "control": control, "spectrum": spectrum, "row_scale": row_scale, "precision": precision, "innovation": innovation}


def hartley(field, axis):
    length = field.shape[axis]
    spectral = jnp.fft.fft(field, axis=axis)
    return (spectral.real - spectral.imag) / math.sqrt(length)

def localize(fields, spectrum):
    first = hartley(hartley(fields, 3), 2)
    first = first * jnp.swapaxes(spectrum, 1, 2)[None]
    return hartley(hartley(first, 3), 2)

def reference(ensemble, control, spectrum, row_scale, precision, innovation):
    members = ensemble.astype(jnp.float32)
    alpha = localize(control, spectrum)
    scale = row_scale[:, :, None] / math.sqrt(MEMBERS - 1)
    increment = scale * lax.optimization_barrier(jnp.sum(members * alpha, axis=0))
    weighted = precision * (increment - innovation)
    return control + localize(members * (scale * weighted)[None], spectrum)
```

```python
import functools
import math

import jax
import jax.numpy as jnp
import ml_dtypes
import numpy as np
from jax import lax
from jax.experimental import pallas as pl
from jax.experimental.pallas import tpu as pltpu
from jax.sharding import PartitionSpec as P

MESH = pl.DeviceIdType.MESH
SPZ, SPG, C, E, GX, RS1, RS2, WZ, WG, AX, G = range(11)


def hartley_matrix(n):
    index = np.arange(n, dtype=np.int64)
    angle = (index[:, None] * index[None, :] % n) * (2.0 * math.pi / n)
    return (np.cos(angle) + np.sin(angle)) / math.sqrt(n)


def two_parts(table):
    high = table.astype(ml_dtypes.bfloat16)
    low = (table - high.astype(np.float64)).astype(ml_dtypes.bfloat16)
    return np.stack([high, low])


def dot(a, b):
    return jnp.dot(a, b, preferred_element_type=jnp.float32)


def parts_of(x):
    high = x.astype(jnp.bfloat16)
    return high, (x - high.astype(jnp.float32)).astype(jnp.bfloat16)


def times_table(x, table):
    high, low = parts_of(x)
    return dot(high, table[0]) + dot(low, table[0]) + dot(high, table[1])


def table_times(table, k, y):
    high, low = parts_of(y)
    width = y.shape[1]
    both = dot(table[k, 0], jnp.concatenate([high, low], axis=1))
    return both[:, :width] + both[:, width:] + dot(table[k, 1], high)


def kernel(
    zn, jn, factor,
    ctrl, ens, spec, rscale, prec, innov, col, icol, row_hbm,
    out,
    row, cst, crecv, e32, erecv, specz, specg, spect, field, gx, prod, rs1, part, rs2, wz, wg, adj, adjc, ax, gout, grecv,
    send, recv, local_sem,
):
    mn, _, rn, ny = ctrl.shape
    nx = spec.shape[2]
    kb = spec.shape[1] // 2
    kc = ny // 4
    hr = rn // 2
    half = nx // 2
    an, bn = prod.shape[1] // (ny // prod.shape[4]), ny // prod.shape[4]
    lw = prod.shape[4]
    px = nx // jn
    ei, si = lax.axis_index("ens"), lax.axis_index("space")
    j, core = lax.div(ei, 2), lax.rem(ei, 2)
    xl, z = lax.div(si, zn), lax.rem(si, zn)
    q = xl * 2 + core
    owner_core = lax.div(z, mn)
    member = lax.rem(z, mn)
    in_plane_set = owner_core == core

    def dev(j_, xl_, core_, z_):
        return (j_ * 2 + core_, xl_ * zn + z_)

    def remote(src, dst, phase, l, device):
        return pltpu.make_async_remote_copy(
            src_ref=src, dst_ref=dst, send_sem=send.at[phase, l], recv_sem=recv.at[phase, l],
            device_id=device, device_id_type=MESH,
        )

    def wait(sem, ref):
        pltpu.make_async_copy(ref, ref, sem).wait()

    barrier = pltpu.get_barrier_semaphore()
    mine = q * zn + z

    def greet_group(t, _):
        other = lax.rem(mine + t, 4 * zn)
        oq, oz = lax.div(other, zn), lax.rem(other, zn)
        pl.semaphore_signal(barrier, inc=1, device_id=dev(j, lax.div(oq, 2), lax.rem(oq, 2), oz), device_id_type=MESH)
        return 0

    lax.fori_loop(1, 4 * zn, greet_group, 0)

    def greet_others(t, _):
        pl.semaphore_signal(barrier, inc=1, device_id=dev(lax.rem(j + t, jn), xl, core, z), device_id_type=MESH)
        return 0

    lax.fori_loop(1, jn, greet_others, 0)
    row_copy = pltpu.make_async_copy(row_hbm, row, local_sem)
    row_copy.start()

    def prepare(l, _):
        x = ctrl[:, l].reshape(mn * rn, ny)
        y = times_table(x, col)
        for k in range(4):
            cst[l, :, k] = y[:, k * kc : (k + 1) * kc].reshape(mn, rn, kc)
        for m in range(mn):
            e32[l, m] = ens[m, l].astype(jnp.float32).reshape(2, an, 8, ny)
        return 0

    lax.fori_loop(0, 2, prepare, 0)
    core_k = pl.multiple_of(core * kb, kb)
    piece = pl.multiple_of(j * px, px)
    specz[:, z] = spec[:, pl.ds(core_k, kb), pl.ds(piece, px)]

    pl.semaphore_wait(barrier, 4 * zn - 1 + jn - 1)

    def send_spec(t, _):
        remote(specz.at[:, z], specz.at[:, z], SPZ, 0, dev(j, xl, core, lax.rem(z + t, zn))).start()
        return 0

    lax.fori_loop(1, zn, send_spec, 0)

    def either(same, src, dst, phase, l, device):
        @pl.when(same)
        def _():
            pltpu.make_async_copy(src, dst, recv.at[phase, l]).start()

        @pl.when(jnp.logical_not(same))
        def _():
            remote(src, dst, phase, l, device).start()

    def send_inputs(l, _):
        def send_c(t, _):
            m = lax.rem(lax.div(t, 4) + z, mn)
            k = lax.rem(t, 4)
            xd, cd, zd = lax.div(k, 2), lax.rem(k, 2), core * mn + m
            same = (k == q) & (zd == z)
            either(same, cst.at[l, m, k], crecv.at[l, xl, z], C, l, dev(j, xd, cd, zd))
            return 0

        lax.fori_loop(0, 4 * mn, send_c, 0)

        def send_e(t, _):
            m = lax.rem(lax.div(t, 2) + z, mn)
            cd, zd = lax.rem(t, 2), core * mn + m
            same = (cd == core) & (zd == z)
            either(same, e32.at[l, m, cd], erecv.at[l, z], E, l, dev(j, xl, cd, zd))
            return 0

        lax.fori_loop(0, 2 * mn, send_e, 0)
        return 0

    lax.fori_loop(0, 2, send_inputs, 0)

    wait(recv.at[SPZ, 0], specz.at[:, pl.ds(0, zn - 1)])

    def to_groups(src, dst, phase, l):
        def one(t, _):
            remote(src, dst, phase, l, dev(lax.rem(j + t, jn), xl, core, z)).start()
            return 0

        lax.fori_loop(1, jn, one, 0)

    to_groups(specz, specg.at[j], SPG, 0)
    specg[j] = specz[...]
    row_copy.wait()
    wait(recv.at[SPG, 0], specg.at[pl.ds(0, jn - 1)])
    for l in range(2):
        for k in range(jn):
            spect[l, k * px : (k + 1) * px] = specg[k, l].reshape(kc, px).T

    def rows(l, y):
        even = table_times(row, 0, y[:half] + y[half:]) * spect[l, pl.ds(0, half, 2), :]
        odd = table_times(row, 1, y[:half] - y[half:]) * spect[l, pl.ds(1, half, 2), :]
        a = table_times(row, 0, even)
        b = table_times(row, 2, odd)
        return a + b, a - b

    def to_plane(src_of, dst, phase, l):
        def one(t, _):
            k = lax.rem(q + t, 4)
            xd, cd = lax.div(k, 2), lax.rem(k, 2)
            remote(src_of(k, xd, cd), dst, phase, l, dev(j, xd, cd, z)).start()
            return 0

        lax.fori_loop(1, 4, one, 0)

    def level(l, _):
        wait(recv.at[C, l], crecv.at[l])
        top, bottom = rows(l, crecv[l].reshape(nx, kc))
        field[l, 0] = top.reshape(zn, 2, hr, kc)
        field[l, 1] = bottom.reshape(zn, 2, hr, kc)
        to_plane(lambda k, xd, cd: field.at[l, xd, :, cd], gx.at[l, q], GX, l)
        gx[l, q] = field[l, xl, :, core]
        wait(recv.at[GX, l], gx.at[l, pl.ds(0, 3)])
        x = jnp.concatenate([gx[l, k].reshape(zn * hr, kc) for k in range(4)], axis=1)
        alpha = times_table(x, icol).reshape(zn, an, 8, ny)
        wait(recv.at[E, l], erecv.at[l])
        for a in range(an):
            for b in range(bn):
                lanes = slice(b * lw, (b + 1) * lw)
                prod[l, a * bn + b] = alpha[:, a, :, lanes] * erecv[l, :, a, :, lanes]

        def to_group(t, _):
            jd = lax.rem(j + t, jn)
            remote(prod.at[l, jd], rs1.at[l, j], RS1, l, dev(jd, xl, core, z)).start()
            return 0

        lax.fori_loop(1, jn, to_group, 0)
        rs1[l, j] = prod[l, j]
        wait(recv.at[RS1, l], rs1.at[l, pl.ds(0, jn - 1)])
        part[l] = jnp.sum(rs1[l], axis=0)

        def to_z(t, _):
            zd = lax.rem(z + t, zn)
            remote(part.at[l, zd], rs2.at[l, z], RS2, l, dev(j, xl, core, zd)).start()
            return 0

        lax.fori_loop(1, zn, to_z, 0)
        rs2[l, z] = part[l, z]
        wait(recv.at[RS2, l], rs2.at[l, pl.ds(0, zn - 1)])
        total = jnp.sum(rs2[l], axis=0)

        first = core * hr + lax.div(j, bn) * 8
        first = pl.multiple_of(first, 8)
        lane = pl.multiple_of(lax.rem(j, bn) * lw, lw)
        here = lax.broadcasted_iota(jnp.int32, (8, rn), 0) + first == lax.broadcasted_iota(jnp.int32, (8, rn), 1)
        scale = jnp.sum(jnp.where(here, rscale[pl.ds(l, 1), :], 0.0), axis=1, keepdims=True) * factor
        weighted = prec[l, pl.ds(first, 8), pl.ds(lane, lw)] * (
            scale * total - innov[l, pl.ds(first, 8), pl.ds(lane, lw)]
        )
        wz[l, z] = scale * weighted

        def w_to_z(t, _):
            remote(wz.at[l, z], wz.at[l, z], WZ, l, dev(j, xl, core, lax.rem(z + t, zn))).start()
            return 0

        lax.fori_loop(1, zn, w_to_z, 0)
        wait(recv.at[WZ, l], wz.at[l, pl.ds(0, zn - 1)])
        to_groups(wz.at[l], wg.at[l, j], WG, l)
        wg[l, j] = wz[l]
        wait(recv.at[WG, l], wg.at[l, pl.ds(0, jn - 1)])

        for a in range(an):
            for b in range(bn):
                lanes = slice(b * lw, (b + 1) * lw)
                adj[:, a, :, lanes] = wg[l, a * bn + b] * erecv[l, :, a, :, lanes]
        y = times_table(adj[...].reshape(zn * hr, ny), col)
        for k in range(4):
            adjc[l, k] = y[:, k * kc : (k + 1) * kc].reshape(zn, hr, kc)
        to_plane(lambda k, xd, cd: adjc.at[l, k], ax.at[l, xl, :, core], AX, l)
        ax[l, xl, :, core] = adjc[l, q]
        wait(recv.at[AX, l], adjc.at[l, pl.ds(0, 3)])
        top, bottom = rows(l, ax[l].reshape(nx, kc))
        gout[l, 0] = top.reshape(zn, rn, kc)
        gout[l, 1] = bottom.reshape(zn, rn, kc)

        def send_g(t, _):
            xd = lax.rem(t, 2)
            zd = lax.rem(lax.div(t, 2) + z, zn)
            same = in_plane_set & (xd == xl) & (zd == z)
            either(same, gout.at[l, xd, zd], grecv.at[l, member, q], G, l, dev(j, xd, owner_core, zd))
            return 0

        lax.fori_loop(0, 2 * zn, send_g, 0)
        return 0

    lax.fori_loop(0, 2, level, 0)

    def finish(l, _):
        wait(recv.at[G, l], grecv.at[l])
        x = jnp.concatenate([grecv[l, :, k].reshape(mn * rn, kc) for k in range(4)], axis=1)
        out[:, l] = ctrl[:, l] + times_table(x, icol).reshape(mn, rn, ny)
        return 0

    lax.fori_loop(0, 2, finish, 0)

    wait(send.at[SPZ, 0], specz.at[:, pl.ds(0, zn - 1)])
    wait(send.at[SPG, 0], specg.at[pl.ds(0, jn - 1)])

    def sent(l, _):
        wait(send.at[GX, l], gx.at[l, pl.ds(0, 3)])
        wait(send.at[AX, l], adjc.at[l, pl.ds(0, 3)])
        wait(send.at[RS1, l], rs1.at[l, pl.ds(0, jn - 1)])
        wait(send.at[WG, l], wg.at[l, pl.ds(0, jn - 1)])
        wait(send.at[RS2, l], rs2.at[l, pl.ds(0, zn - 1)])
        wait(send.at[WZ, l], wz.at[l, pl.ds(0, zn - 1)])

        @pl.when(in_plane_set)
        def _():
            wait(send.at[C, l], crecv.at[l, 0])
            wait(send.at[C, l], crecv.at[l, 1, pl.ds(0, zn - 1)])
            wait(send.at[E, l], erecv.at[l, pl.ds(0, zn - 1)])
            wait(send.at[G, l], gout.at[l, 0])
            wait(send.at[G, l], gout.at[l, 1, pl.ds(0, zn - 1)])

        @pl.when(jnp.logical_not(in_plane_set))
        def _():
            wait(send.at[C, l], crecv.at[l])
            wait(send.at[E, l], erecv.at[l])
            wait(send.at[G, l], gout.at[l])

        return 0

    lax.fori_loop(0, 2, sent, 0)


def body(zn, jn, members_all, interpret_lanes, ensemble, control, spectrum, row_scale, precision, innovation):
    mn, _, rn, ny = control.shape
    nx = spectrum.shape[2]
    kb = spectrum.shape[1] // 2
    kc, hr, px = ny // 4, rn // 2, nx // jn
    lw = interpret_lanes
    an = hr // 8
    assert mn * 2 == zn and an * (ny // lw) == jn and kb * zn == kc
    h_col, h_row = hartley_matrix(ny), hartley_matrix(nx)
    k = np.arange(ny).reshape(2, zn, 2, kb).transpose(0, 2, 1, 3).reshape(-1)
    col, icol = two_parts(h_col[:, k]), two_parts(h_col[k, :])
    even, odd = h_row[0::2, : nx // 2], h_row[1::2, : nx // 2]
    row = np.stack([two_parts(even), two_parts(odd), two_parts(odd.T)])
    f32 = jnp.float32
    vmem, anyspace = pl.BlockSpec(memory_space=pltpu.VMEM), pl.BlockSpec(memory_space=pl.ANY)
    return pl.pallas_call(
        functools.partial(kernel, zn, jn, 1.0 / math.sqrt(members_all - 1)),
        out_shape=jax.ShapeDtypeStruct(control.shape, f32),
        in_specs=[vmem] * 8 + [anyspace],
        out_specs=vmem,
        scratch_shapes=[
            pltpu.VMEM(row.shape, jnp.bfloat16),
            pltpu.VMEM((2, mn, 4, rn, kc), f32),
            pltpu.VMEM((2, 2, zn, rn, kc), f32),
            pltpu.VMEM((2, mn, 2, an, 8, ny), f32),
            pltpu.VMEM((2, zn, an, 8, ny), f32),
            pltpu.VMEM((2, zn, kb, px), f32),
            pltpu.VMEM((jn, 2, zn, kb, px), f32),
            pltpu.VMEM((2, nx, kc), f32),
            pltpu.VMEM((2, 2, zn, 2, hr, kc), f32),
            pltpu.VMEM((2, 4, zn, hr, kc), f32),
            pltpu.VMEM((2, jn, zn, 8, lw), f32),
            pltpu.VMEM((2, jn, zn, 8, lw), f32),
            pltpu.VMEM((2, zn, 8, lw), f32),
            pltpu.VMEM((2, zn, 8, lw), f32),
            pltpu.VMEM((2, zn, 8, lw), f32),
            pltpu.VMEM((2, jn, zn, 8, lw), f32),
            pltpu.VMEM((zn, an, 8, ny), f32),
            pltpu.VMEM((2, 4, zn, hr, kc), f32),
            pltpu.VMEM((2, 2, zn, 2, hr, kc), f32),
            pltpu.VMEM((2, 2, zn, rn, kc), f32),
            pltpu.VMEM((2, mn, 4, rn, kc), f32),
            pltpu.SemaphoreType.DMA((11, 2)),
            pltpu.SemaphoreType.DMA((11, 2)),
            pltpu.SemaphoreType.DMA,
        ],
        compiler_params=pltpu.CompilerParams(
            collective_id=0, has_side_effects=True, vmem_limit_bytes=50 * 1024 * 1024
        ),
        name="gradient",
    )(control, ensemble, spectrum, row_scale, precision, innovation, jnp.asarray(col), jnp.asarray(icol), jnp.asarray(row))


def solution(mesh, lanes=128):
    zn, jn = mesh.shape["space"] // 2, mesh.shape["ens"] // 2
    in_specs = (
        P("ens", None, "space", None),
        P("ens", None, "space", None),
        P(None, "space", None),
        P(None, "space"),
        P(None, "space", None),
        P(None, "space", None),
    )
    out_specs = P("ens", None, "space", None)

    def whole(ensemble, *rest):
        step = functools.partial(body, zn, jn, ensemble.shape[0], lanes)
        return jax.shard_map(step, mesh=mesh, in_specs=in_specs, out_specs=out_specs, check_vma=False)(ensemble, *rest)

    return whole
```

```python
import functools
import math

import jax
import jax.numpy as jnp
import ml_dtypes
import numpy as np
from jax import lax
from jax.experimental import pallas as pl
from jax.experimental.pallas import tpu as pltpu
from jax.sharding import PartitionSpec as P

MESH = pl.DeviceIdType.MESH
SPZ, SPG, C, E, GX, RS1, RS2, WZ, WG, AX, G = range(11)
FEED = ((2, 4, 9, 20, 32), (2, 3, 6, 16, 16))


def hartley_matrix(n):
    index = np.arange(n, dtype=np.int64)
    angle = (index[:, None] * index[None, :] % n) * (2.0 * math.pi / n)
    return (np.cos(angle) + np.sin(angle)) / math.sqrt(n)


def two_parts(table):
    high = table.astype(ml_dtypes.bfloat16)
    low = (table - high.astype(np.float64)).astype(ml_dtypes.bfloat16)
    return np.stack([high, low])


def dot(a, b):
    return jnp.dot(a, b, preferred_element_type=jnp.float32)


def parts_of(x):
    high = x.astype(jnp.bfloat16)
    return high, (x - high.astype(jnp.float32)).astype(jnp.bfloat16)


def times_table(x, table):
    high, low = parts_of(x)
    return dot(high, table[0]) + dot(low, table[0]) + dot(high, table[1])


def table_times(table, k, y):
    high, low = parts_of(y)
    width = y.shape[1]
    both = dot(table[k, 0], jnp.concatenate([high, low], axis=1))
    return both[:, :width] + both[:, width:] + dot(table[k, 1], high)


def kernel(
    zn, jn, factor,
    ctrl_hbm, ens_hbm, spec_hbm, rscale_hbm, prec_hbm, innov_hbm, col_hbm, icol_hbm, row_hbm,
    out,
    ctrl, ens, spec, rscale, prec, innov, col, icol, row,
    cst, crecv, e32, erecv, specz, specg, spect, field, gx, alpha, prod, rs1, part, rs2, wz, wg, adj, adjc, ax, nat, gout,
    grecv, send, recv, local_sem,
):
    mn, _, rn, ny = ctrl.shape
    nx = spec.shape[2]
    kb = spec.shape[1] // 2
    kc = ny // 4
    hr = rn // 2
    half = nx // 2
    lw = prod.shape[4]
    bn = ny // lw
    an = jn // bn
    px = nx // jn
    chunks = min(4, zn)
    cs = zn // chunks
    ei, si = lax.axis_index("ens"), lax.axis_index("space")
    j, core = lax.div(ei, 2), lax.rem(ei, 2)
    xl, z = lax.div(si, zn), lax.rem(si, zn)
    q = xl * 2 + core
    owner_core = lax.div(z, mn)
    member = lax.rem(z, mn)
    in_plane_set = owner_core == core

    def dev(j_, xl_, core_, z_):
        return (j_ * 2 + core_, xl_ * zn + z_)

    def remote(src, dst, phase, l, device, c=0):
        return pltpu.make_async_remote_copy(
            src_ref=src, dst_ref=dst, send_sem=send.at[phase, l], recv_sem=recv.at[phase, l, c],
            device_id=device, device_id_type=MESH,
        )

    def wait(sem, ref):
        pltpu.make_async_copy(ref, ref, sem).wait()

    def offset(p):
        far = lax.div(zn - p, 2)
        return jnp.where(lax.rem(p, 2) == 1, far, -far)

    def plane_of(p):
        return lax.rem(z + offset(p) + zn, zn)

    def plane_back(p):
        return lax.rem(z - offset(p) + zn, zn)

    loads = [
        pltpu.make_async_copy(src, dst, local_sem.at[i])
        for i, (src, dst) in enumerate(
            [
                (ctrl_hbm.at[:, 0], ctrl.at[:, 0]), (col_hbm, col), (spec_hbm, spec), (ens_hbm, ens),
                (ctrl_hbm.at[:, 1], ctrl.at[:, 1]), (row_hbm, row), (icol_hbm, icol), (rscale_hbm, rscale),
                (prec_hbm, prec), (innov_hbm, innov),
            ]
        )
    ]
    barrier = pltpu.get_barrier_semaphore()
    mine = q * zn + z

    def greet_group(t, _):
        other = lax.rem(mine + t, 4 * zn)
        oq, oz = lax.div(other, zn), lax.rem(other, zn)
        pl.semaphore_signal(barrier, inc=1, device_id=dev(j, lax.div(oq, 2), lax.rem(oq, 2), oz), device_id_type=MESH)
        return 0

    lax.fori_loop(1, 4 * zn, greet_group, 0)

    def greet_others(t, _):
        pl.semaphore_signal(barrier, inc=1, device_id=dev(lax.rem(j + t, jn), xl, core, z), device_id_type=MESH)
        return 0

    lax.fori_loop(1, jn, greet_others, 0)
    for load in loads[:5]:
        load.start()

    def columns(l):
        y = times_table(ctrl[:, l].reshape(mn * rn, ny), col)
        for k in range(4):
            cst[l, :, k] = y[:, k * kc : (k + 1) * kc].reshape(mn, rn, kc)

    def widen(l):
        for m in range(mn):
            e32[l, m] = ens[m, l].astype(jnp.float32).reshape(2, an, 8, ny)

    def either(same, src, dst, phase, l, device, c=0):
        @pl.when(same)
        def _():
            pltpu.make_async_copy(src, dst, recv.at[phase, l, c]).start()

        @pl.when(jnp.logical_not(same))
        def _():
            remote(src, dst, phase, l, device, c).start()

    def send_control(l, low, high):
        def one(p, _):
            zd = plane_back(p)

            @pl.when(lax.div(zd, mn) == core)
            def _():
                for k in range(4):
                    remote(cst.at[l, lax.rem(zd, mn), k], crecv.at[l, xl, z], C, l, dev(j, k // 2, k % 2, zd)).start()

            return 0

        lax.fori_loop(low, min(high, zn - 1), one, 0)
        if low < high == zn:

            @pl.when(in_plane_set)
            def _():
                for k in range(4):
                    either(q == k, cst.at[l, member, k], crecv.at[l, xl, z], C, l, dev(j, k // 2, k % 2, z))

    def send_ensemble(l, low, high):
        def one(p, _):
            zd = plane_back(p)

            @pl.when(lax.div(zd, mn) == core)
            def _():
                for k in range(2):
                    remote(
                        e32.at[l, lax.rem(zd, mn), k], erecv.at[l, p], E, l, dev(j, xl, k, zd), lax.div(p, cs)
                    ).start()

            return 0

        lax.fori_loop(low, min(high, zn - 1), one, 0)
        if low < high == zn:

            @pl.when(in_plane_set)
            def _():
                for k in range(2):
                    either(core == k, e32.at[l, member, k], erecv.at[l, zn - 1], E, l, dev(j, xl, k, z), chunks - 1)

    def send_gradient(l, low, high):
        def one(p, _):
            zd = plane_back(p)
            for k in range(2):
                remote(gout.at[l, k, zd], grecv.at[l, member, q], G, l, dev(j, k, owner_core, zd)).start()
            return 0

        lax.fori_loop(low, min(high, zn - 1), one, 0)
        if low < high == zn:
            for k in range(2):
                either(
                    in_plane_set & (xl == k), gout.at[l, k, z], grecv.at[l, member, q], G, l, dev(j, k, owner_core, z)
                )

    def to_groups(src_of, dst, phase, l, c=0):
        def one(t, _):
            jd = lax.rem(j + t, jn)
            remote(src_of(jd), dst, phase, l, dev(jd, xl, core, z), c).start()
            return 0

        lax.fori_loop(1, jn, one, 0)

    def to_plane(src_of, dst, phase, l, c=0):
        def one(t, _):
            k = lax.rem(q + t, 4)
            xd, cd = lax.div(k, 2), lax.rem(k, 2)
            remote(src_of(k, xd, cd), dst, phase, l, dev(j, xd, cd, z), c).start()
            return 0

        lax.fori_loop(1, 4, one, 0)

    def rows(l, y):
        even = table_times(row, 0, y[:half] + y[half:]) * spect[l, pl.ds(0, half, 2), :]
        odd = table_times(row, 1, y[:half] - y[half:]) * spect[l, pl.ds(1, half, 2), :]
        a = table_times(row, 0, even)
        b = table_times(row, 2, odd)
        return a + b, a - b

    def start_alpha(l):
        wait(recv.at[C, l, 0], crecv.at[l])
        top, bottom = rows(l, crecv[l].reshape(nx, kc))
        field[l, 0] = top.reshape(zn, 2, hr, kc)
        field[l, 1] = bottom.reshape(zn, 2, hr, kc)
        to_plane(lambda k, xd, cd: field.at[l, xd, :, cd], gx.at[l, q], GX, l)
        gx[l, q] = field[l, xl, :, core]

    def make_alpha(l):
        wait(recv.at[GX, l, 0], gx.at[l, pl.ds(0, 3)])
        x = jnp.concatenate([gx[l, k].reshape(zn * hr, kc) for k in range(4)], axis=1)
        alpha[l] = times_table(x, icol).reshape(zn, an, 8, ny)

    def feed(l, point):
        low = FEED[l][point - 1] * zn // 16 if point else 0
        high = FEED[l][point] * zn // 16
        if l == 0:
            send_control(1, min(low, zn), min(high, zn))
            send_ensemble(1, max(low - zn, 0), max(high - zn, 0))
        else:
            send_gradient(0, low, high)

    def sum_groups(l, c):
        low, high = c * cs, (c + 1) * cs
        wait(recv.at[RS1, l, c], rs1.at[l, pl.ds(0, jn - 1), pl.ds(low, cs)])
        part[l, low:high] = jnp.sum(rs1[l, :, low:high], axis=0)

        def one(p, _):
            remote(part.at[l, p], rs2.at[l, p], RS2, l, dev(j, xl, core, plane_of(p))).start()
            return 0

        lax.fori_loop(low, min(high, zn - 1), one, 0)

    def sum_members(l):
        for c in range(chunks):
            low = c * cs
            if c >= chunks - 2:
                feed(l, c - (chunks - 2))
            wait(recv.at[E, l, c], erecv.at[l, pl.ds(low, cs)])

            def multiply(p, _):
                here = plane_of(p)
                for a in range(an):
                    for b in range(bn):
                        lanes = slice(b * lw, (b + 1) * lw)
                        prod[l, a * bn + b, p] = alpha[l, here, a, :, lanes] * erecv[l, p, a, :, lanes]
                return 0

            lax.fori_loop(low, low + cs, multiply, 0)
            to_groups(lambda jd: prod.at[l, jd, pl.ds(low, cs)], rs1.at[l, j, pl.ds(low, cs)], RS1, l, c)
            rs1[l, j, low : low + cs] = prod[l, j, low : low + cs]
            if c > 0:
                sum_groups(l, c - 1)
        sum_groups(l, chunks - 1)
        rs2[l, zn - 1] = part[l, zn - 1]

    def make_factor(l):
        wait(recv.at[RS2, l, 0], rs2.at[l, pl.ds(0, zn - 1)])
        total = jnp.sum(rs2[l], axis=0)
        first = pl.multiple_of(core * hr + lax.div(j, bn) * 8, 8)
        lane = pl.multiple_of(lax.rem(j, bn) * lw, lw)
        here = lax.broadcasted_iota(jnp.int32, (8, rn), 0) + first == lax.broadcasted_iota(jnp.int32, (8, rn), 1)
        scale = jnp.sum(jnp.where(here, rscale[l : l + 1, :], 0.0), axis=1, keepdims=True) * factor
        weighted = prec[l, pl.ds(first, 8), pl.ds(lane, lw)] * (
            scale * total - innov[l, pl.ds(first, 8), pl.ds(lane, lw)]
        )
        wz[l, zn - 1] = scale * weighted

        def one(p, _):
            remote(wz.at[l, zn - 1], wz.at[l, p], WZ, l, dev(j, xl, core, plane_back(p)), lax.div(p, cs)).start()
            return 0

        lax.fori_loop(0, zn - 1, one, 0)

    def spread_factor(l):
        for c in reversed(range(chunks)):
            low = c * cs
            others = cs - 1 if c == chunks - 1 else cs
            if others:
                wait(recv.at[WZ, l, c], wz.at[l, pl.ds(0, others)])
            to_groups(lambda jd: wz.at[l, pl.ds(low, cs)], wg.at[l, j, pl.ds(low, cs)], WG, l, c)
            wg[l, j, low : low + cs] = wz[l, low : low + cs]

    def start_adjoint(l):
        hs = zn // 2
        for h in (1, 0):
            low = h * hs
            for c in reversed(range(h * chunks // 2, (h + 1) * chunks // 2)):
                wait(recv.at[WG, l, c], wg.at[l, pl.ds(0, jn - 1), pl.ds(c * cs, cs)])
            for a in range(an):
                for b in range(bn):
                    lanes = slice(b * lw, (b + 1) * lw)
                    adj[low : low + hs, a, :, lanes] = (
                        wg[l, a * bn + b, low : low + hs] * erecv[l, low : low + hs, a, :, lanes]
                    )
            y = times_table(adj[low : low + hs].reshape(hs * hr, ny), col)
            for k in range(4):
                adjc[l, k, low : low + hs] = y[:, k * kc : (k + 1) * kc].reshape(hs, hr, kc)
            to_plane(
                lambda k, xd, cd: adjc.at[l, k, pl.ds(low, hs)], ax.at[l, xl, pl.ds(low, hs), core], AX, l, h
            )
            ax[l, xl, low : low + hs, core] = adjc[l, q, low : low + hs]

    def adjoint(l):
        hs = zn // 2
        for h in (1, 0):
            wait(recv.at[AX, l, h], adjc.at[l, pl.ds(0, 3), pl.ds(0, hs)])

        def place(p, _):
            nat[:, plane_of(p)] = ax[l, :, p]
            return 0

        lax.fori_loop(0, zn, place, 0)
        top, bottom = rows(l, nat[...].reshape(nx, kc))
        gout[l, 0] = top.reshape(zn, rn, kc)
        gout[l, 1] = bottom.reshape(zn, rn, kc)

    def finish(l):
        wait(recv.at[G, l, 0], grecv.at[l])
        x = jnp.concatenate([grecv[l, :, k].reshape(mn * rn, kc) for k in range(4)], axis=1)
        out[:, l] = ctrl[:, l] + times_table(x, icol).reshape(mn, rn, ny)

    loads[0].wait()
    loads[1].wait()
    columns(0)
    loads[2].wait()
    core_k = pl.multiple_of(core * kb, kb)
    piece = pl.multiple_of(j * px, px)
    specz[:, z] = spec[:, pl.ds(core_k, kb), pl.ds(piece, px)]
    pl.semaphore_wait(barrier, 4 * zn - 1 + jn - 1)

    def send_spec(t, _):
        remote(specz.at[:, z], specz.at[:, z], SPZ, 0, dev(j, xl, core, lax.rem(z + t, zn))).start()
        return 0

    lax.fori_loop(1, zn, send_spec, 0)
    send_control(0, 0, zn)
    loads[3].wait()
    widen(0)
    send_ensemble(0, 0, zn)
    for load in loads[5:]:
        load.start()
    loads[4].wait()
    columns(1)
    widen(1)
    for load in loads[5:]:
        load.wait()

    wait(recv.at[SPZ, 0, 0], specz.at[:, pl.ds(0, zn - 1)])
    to_groups(lambda jd: specz, specg.at[j], SPG, 0)
    specg[j] = specz[...]
    wait(recv.at[SPG, 0, 0], specg.at[pl.ds(0, jn - 1)])
    for l in range(2):
        for k in range(jn):
            spect[l, k * px : (k + 1) * px] = specg[k, l].reshape(kc, px).T

    start_alpha(0)
    make_alpha(0)
    for l in range(2):
        sum_members(l)
        feed(l, 2)
        make_factor(l)
        feed(l, 3)
        spread_factor(l)
        feed(l, 4)
        if l == 0:
            start_alpha(1)
        start_adjoint(l)
        if l == 0:
            make_alpha(1)
        adjoint(l)
    send_gradient(1, 0, zn)
    finish(0)
    finish(1)

    wait(send.at[SPZ, 0], specz.at[:, pl.ds(0, zn - 1)])
    wait(send.at[SPG, 0], specg.at[pl.ds(0, jn - 1)])

    def sent(l, _):
        wait(send.at[GX, l], gx.at[l, pl.ds(0, 3)])
        wait(send.at[AX, l], adjc.at[l, pl.ds(0, 3)])
        wait(send.at[RS1, l], rs1.at[l, pl.ds(0, jn - 1)])
        wait(send.at[WG, l], wg.at[l, pl.ds(0, jn - 1)])
        wait(send.at[RS2, l], rs2.at[l, pl.ds(0, zn - 1)])
        wait(send.at[WZ, l], wz.at[l, pl.ds(0, zn - 1)])

        @pl.when(in_plane_set)
        def _():
            wait(send.at[C, l], crecv.at[l, 0])
            wait(send.at[C, l], crecv.at[l, 1, pl.ds(0, zn - 1)])
            wait(send.at[E, l], erecv.at[l, pl.ds(0, zn - 1)])
            wait(send.at[G, l], gout.at[l, 0])
            wait(send.at[G, l], gout.at[l, 1, pl.ds(0, zn - 1)])

        @pl.when(jnp.logical_not(in_plane_set))
        def _():
            wait(send.at[C, l], crecv.at[l])
            wait(send.at[E, l], erecv.at[l])
            wait(send.at[G, l], gout.at[l])

        return 0

    lax.fori_loop(0, 2, sent, 0)


def body(zn, jn, members_all, interpret_lanes, ensemble, control, spectrum, row_scale, precision, innovation):
    mn, _, rn, ny = control.shape
    nx = spectrum.shape[2]
    kb = spectrum.shape[1] // 2
    kc, hr, px = ny // 4, rn // 2, nx // jn
    lw = interpret_lanes
    an = hr // 8
    assert mn * 2 == zn and an * (ny // lw) == jn and kb * zn == kc
    h_col, h_row = hartley_matrix(ny), hartley_matrix(nx)
    k = np.arange(ny).reshape(2, zn, 2, kb).transpose(0, 2, 1, 3).reshape(-1)
    col, icol = two_parts(h_col[:, k]), two_parts(h_col[k, :])
    even, odd = h_row[0::2, : nx // 2], h_row[1::2, : nx // 2]
    row = np.stack([two_parts(even), two_parts(odd), two_parts(odd.T)])
    f32 = jnp.float32
    vmem, anyspace = pl.BlockSpec(memory_space=pltpu.VMEM), pl.BlockSpec(memory_space=pl.ANY)
    return pl.pallas_call(
        functools.partial(kernel, zn, jn, 1.0 / math.sqrt(members_all - 1)),
        out_shape=jax.ShapeDtypeStruct(control.shape, f32),
        in_specs=[anyspace] * 9,
        out_specs=vmem,
        scratch_shapes=[
            pltpu.VMEM(control.shape, f32),
            pltpu.VMEM(ensemble.shape, ensemble.dtype),
            pltpu.VMEM(spectrum.shape, f32),
            pltpu.VMEM(row_scale.shape, f32),
            pltpu.VMEM(precision.shape, f32),
            pltpu.VMEM(innovation.shape, f32),
            pltpu.VMEM(col.shape, jnp.bfloat16),
            pltpu.VMEM(icol.shape, jnp.bfloat16),
            pltpu.VMEM(row.shape, jnp.bfloat16),
            pltpu.VMEM((2, mn, 4, rn, kc), f32),
            pltpu.VMEM((2, 2, zn, rn, kc), f32),
            pltpu.VMEM((2, mn, 2, an, 8, ny), f32),
            pltpu.VMEM((2, zn, an, 8, ny), f32),
            pltpu.VMEM((2, zn, kb, px), f32),
            pltpu.VMEM((jn, 2, zn, kb, px), f32),
            pltpu.VMEM((2, nx, kc), f32),
            pltpu.VMEM((2, 2, zn, 2, hr, kc), f32),
            pltpu.VMEM((2, 4, zn, hr, kc), f32),
            pltpu.VMEM((2, zn, an, 8, ny), f32),
            pltpu.VMEM((2, jn, zn, 8, lw), f32),
            pltpu.VMEM((2, jn, zn, 8, lw), f32),
            pltpu.VMEM((2, zn, 8, lw), f32),
            pltpu.VMEM((2, zn, 8, lw), f32),
            pltpu.VMEM((2, zn, 8, lw), f32),
            pltpu.VMEM((2, jn, zn, 8, lw), f32),
            pltpu.VMEM((zn, an, 8, ny), f32),
            pltpu.VMEM((2, 4, zn, hr, kc), f32),
            pltpu.VMEM((2, 2, zn, 2, hr, kc), f32),
            pltpu.VMEM((2, zn, 2, hr, kc), f32),
            pltpu.VMEM((2, 2, zn, rn, kc), f32),
            pltpu.VMEM((2, mn, 4, rn, kc), f32),
            pltpu.SemaphoreType.DMA((11, 2)),
            pltpu.SemaphoreType.DMA((11, 2, 4)),
            pltpu.SemaphoreType.DMA((10,)),
        ],
        compiler_params=pltpu.CompilerParams(
            collective_id=0, has_side_effects=True, vmem_limit_bytes=50 * 1024 * 1024
        ),
        name="gradient",
    )(control, ensemble, spectrum, row_scale, precision, innovation, jnp.asarray(col), jnp.asarray(icol), jnp.asarray(row))


def solution(mesh, lanes=128):
    zn, jn = mesh.shape["space"] // 2, mesh.shape["ens"] // 2
    in_specs = (
        P("ens", None, "space", None),
        P("ens", None, "space", None),
        P(None, "space", None),
        P(None, "space"),
        P(None, "space", None),
        P(None, "space", None),
    )
    out_specs = P("ens", None, "space", None)

    def whole(ensemble, *rest):
        step = functools.partial(body, zn, jn, ensemble.shape[0], lanes)
        return jax.shard_map(step, mesh=mesh, in_specs=in_specs, out_specs=out_specs, check_vma=False)(ensemble, *rest)

    return whole
```

```python
import functools
import math

import jax
import jax.numpy as jnp
import ml_dtypes
import numpy as np
from jax import lax
from jax.experimental import pallas as pl
from jax.experimental.pallas import tpu as pltpu
from jax.sharding import PartitionSpec as P

MESH = pl.DeviceIdType.MESH
SPZ, SPG, C, E, GX, RS1, RS2, WZ, WG, AX, G = range(11)
FEED = ((4, 6, 12, 32, 32), (0, 0, 0, 16, 16))


def hartley_matrix(n):
    index = np.arange(n, dtype=np.int64)
    angle = (index[:, None] * index[None, :] % n) * (2.0 * math.pi / n)
    return (np.cos(angle) + np.sin(angle)) / math.sqrt(n)


def two_parts(table):
    high = table.astype(ml_dtypes.bfloat16)
    low = (table - high.astype(np.float64)).astype(ml_dtypes.bfloat16)
    return np.stack([high, low])


def dot(a, b):
    return jnp.dot(a, b, preferred_element_type=jnp.float32)


def parts_of(x):
    high = x.astype(jnp.bfloat16)
    return high, (x - high.astype(jnp.float32)).astype(jnp.bfloat16)


def times_table(x, table):
    high, low = parts_of(x)
    return dot(high, table[0]) + dot(low, table[0]) + dot(high, table[1])


def table_times(table, k, y):
    high, low = parts_of(y)
    width = y.shape[1]
    both = dot(table[k, 0], jnp.concatenate([high, low], axis=1))
    return both[:, :width] + both[:, width:] + dot(table[k, 1], high)


def kernel(
    zn, jn, factor,
    ctrl_hbm, ens_hbm, spec_hbm, rscale_hbm, prec_hbm, innov_hbm, col_hbm, icol_hbm, row_hbm,
    out,
    ctrl, ens, spec, rscale, prec, innov, col, icol, row,
    cst, crecv, e32, erecv, specz, specg, spect, field, gx, alpha, prod, rs1, part, rs2, wz, wg, adj, adjc, ax, nat, gout,
    grecv, send, recv, local_sem,
):
    mn, _, rn, ny = ctrl.shape
    nx = spec.shape[2]
    kb = spec.shape[1] // 2
    kc = ny // 4
    hr = rn // 2
    half = nx // 2
    lw = prod.shape[4]
    bn = ny // lw
    an = jn // bn
    px = nx // jn
    chunks = min(2, zn)
    cs = zn // chunks
    ei, si = lax.axis_index("ens"), lax.axis_index("space")
    j, core = lax.div(ei, 2), lax.rem(ei, 2)
    xl, z = lax.div(si, zn), lax.rem(si, zn)
    q = xl * 2 + core
    owner_core = lax.div(z, mn)
    member = lax.rem(z, mn)
    in_plane_set = owner_core == core

    def dev(j_, xl_, core_, z_):
        return (j_ * 2 + core_, xl_ * zn + z_)

    def remote(src, dst, phase, l, device, c=0):
        return pltpu.make_async_remote_copy(
            src_ref=src, dst_ref=dst, send_sem=send.at[phase, l], recv_sem=recv.at[phase, l, c],
            device_id=device, device_id_type=MESH,
        )

    def wait(sem, ref):
        pltpu.make_async_copy(ref, ref, sem).wait()

    def offset(p):
        far = lax.div(zn - p, 2)
        return jnp.where(lax.rem(p, 2) == 1, far, -far)

    def plane_of(p):
        return lax.rem(z + offset(p) + zn, zn)

    def plane_back(p):
        return lax.rem(z - offset(p) + zn, zn)

    loads = [
        pltpu.make_async_copy(src, dst, local_sem.at[i])
        for i, (src, dst) in enumerate(
            [
                (ctrl_hbm.at[:, 0], ctrl.at[:, 0]), (col_hbm, col), (spec_hbm, spec), (ens_hbm, ens),
                (ctrl_hbm.at[:, 1], ctrl.at[:, 1]), (row_hbm, row), (icol_hbm, icol), (rscale_hbm, rscale),
                (prec_hbm, prec), (innov_hbm, innov),
            ]
        )
    ]
    barrier = pltpu.get_barrier_semaphore()
    mine = q * zn + z

    def greet_group(t, _):
        other = lax.rem(mine + t, 4 * zn)
        oq, oz = lax.div(other, zn), lax.rem(other, zn)
        pl.semaphore_signal(barrier, inc=1, device_id=dev(j, lax.div(oq, 2), lax.rem(oq, 2), oz), device_id_type=MESH)
        return 0

    lax.fori_loop(1, 4 * zn, greet_group, 0)

    def greet_others(t, _):
        pl.semaphore_signal(barrier, inc=1, device_id=dev(lax.rem(j + t, jn), xl, core, z), device_id_type=MESH)
        return 0

    lax.fori_loop(1, jn, greet_others, 0)
    for load in loads[:5]:
        load.start()

    def columns(l):
        y = times_table(ctrl[:, l].reshape(mn * rn, ny), col)
        for k in range(4):
            cst[l, :, k] = y[:, k * kc : (k + 1) * kc].reshape(mn, rn, kc)

    def widen(l):
        for m in range(mn):
            e32[l, m] = ens[m, l].astype(jnp.float32).reshape(2, an, 8, ny)

    def either(same, src, dst, phase, l, device, c=0):
        @pl.when(same)
        def _():
            pltpu.make_async_copy(src, dst, recv.at[phase, l, c]).start()

        @pl.when(jnp.logical_not(same))
        def _():
            remote(src, dst, phase, l, device, c).start()

    def send_control(l, low, high):
        def one(p, _):
            zd = plane_back(p)

            @pl.when(lax.div(zd, mn) == core)
            def _():
                for k in range(4):
                    remote(cst.at[l, lax.rem(zd, mn), k], crecv.at[l, xl, z], C, l, dev(j, k // 2, k % 2, zd)).start()

            return 0

        lax.fori_loop(low, min(high, zn - 1), one, 0)
        if low < high == zn:

            @pl.when(in_plane_set)
            def _():
                for k in range(4):
                    either(q == k, cst.at[l, member, k], crecv.at[l, xl, z], C, l, dev(j, k // 2, k % 2, z))

    def send_ensemble(l, low, high):
        def one(p, _):
            zd = plane_back(p)

            @pl.when(lax.div(zd, mn) == core)
            def _():
                for k in range(2):
                    remote(
                        e32.at[l, lax.rem(zd, mn), k], erecv.at[l, p], E, l, dev(j, xl, k, zd), lax.div(p, cs)
                    ).start()

            return 0

        lax.fori_loop(low, min(high, zn - 1), one, 0)
        if low < high == zn:

            @pl.when(in_plane_set)
            def _():
                for k in range(2):
                    either(core == k, e32.at[l, member, k], erecv.at[l, zn - 1], E, l, dev(j, xl, k, z), chunks - 1)

    def send_gradient(l, low, high):
        def one(p, _):
            zd = plane_back(p)
            for k in range(2):
                remote(gout.at[l, k, zd], grecv.at[l, member, q], G, l, dev(j, k, owner_core, zd)).start()
            return 0

        lax.fori_loop(low, min(high, zn - 1), one, 0)
        if low < high == zn:
            for k in range(2):
                either(
                    in_plane_set & (xl == k), gout.at[l, k, z], grecv.at[l, member, q], G, l, dev(j, k, owner_core, z)
                )

    def to_groups(src_of, dst, phase, l, c=0):
        def one(t, _):
            jd = lax.rem(j + t, jn)
            remote(src_of(jd), dst, phase, l, dev(jd, xl, core, z), c).start()
            return 0

        lax.fori_loop(1, jn, one, 0)

    def to_plane(src_of, dst, phase, l, c=0):
        def one(t, _):
            k = lax.rem(q + t, 4)
            xd, cd = lax.div(k, 2), lax.rem(k, 2)
            remote(src_of(k, xd, cd), dst, phase, l, dev(j, xd, cd, z), c).start()
            return 0

        lax.fori_loop(1, 4, one, 0)

    def rows(l, y):
        even = table_times(row, 0, y[:half] + y[half:]) * spect[l, pl.ds(0, half, 2), :]
        odd = table_times(row, 1, y[:half] - y[half:]) * spect[l, pl.ds(1, half, 2), :]
        a = table_times(row, 0, even)
        b = table_times(row, 2, odd)
        return a + b, a - b

    def start_alpha(l):
        wait(recv.at[C, l, 0], crecv.at[l])
        top, bottom = rows(l, crecv[l].reshape(nx, kc))
        field[l, 0] = top.reshape(zn, 2, hr, kc)
        field[l, 1] = bottom.reshape(zn, 2, hr, kc)
        to_plane(lambda k, xd, cd: field.at[l, xd, :, cd], gx.at[l, q], GX, l)
        gx[l, q] = field[l, xl, :, core]

    def make_alpha(l):
        wait(recv.at[GX, l, 0], gx.at[l, pl.ds(0, 3)])
        x = jnp.concatenate([gx[l, k].reshape(zn * hr, kc) for k in range(4)], axis=1)
        alpha[l] = times_table(x, icol).reshape(zn, an, 8, ny)

    def feed(l, point):
        low = FEED[l][point - 1] * zn // 16 if point else 0
        high = FEED[l][point] * zn // 16
        if l == 0:
            send_control(1, min(low, zn), min(high, zn))
            send_ensemble(1, max(low - zn, 0), max(high - zn, 0))
        else:
            send_gradient(0, low, high)

    def sum_groups(l, c):
        low, high = c * cs, (c + 1) * cs
        wait(recv.at[RS1, l, c], rs1.at[l, pl.ds(0, jn - 1), pl.ds(low, cs)])
        part[l, low:high] = jnp.sum(rs1[l, :, low:high], axis=0)

        def one(p, _):
            remote(part.at[l, p], rs2.at[l, p], RS2, l, dev(j, xl, core, plane_of(p))).start()
            return 0

        lax.fori_loop(low, min(high, zn - 1), one, 0)

    def sum_members(l):
        for c in range(chunks):
            low = c * cs
            if c >= chunks - 2:
                feed(l, c - (chunks - 2))
            wait(recv.at[E, l, c], erecv.at[l, pl.ds(low, cs)])

            def multiply(p, _):
                here = plane_of(p)
                for a in range(an):
                    for b in range(bn):
                        lanes = slice(b * lw, (b + 1) * lw)
                        prod[l, a * bn + b, p] = alpha[l, here, a, :, lanes] * erecv[l, p, a, :, lanes]
                return 0

            lax.fori_loop(low, low + cs, multiply, 0)
            to_groups(lambda jd: prod.at[l, jd, pl.ds(low, cs)], rs1.at[l, j, pl.ds(low, cs)], RS1, l, c)
            rs1[l, j, low : low + cs] = prod[l, j, low : low + cs]
            if c > 0:
                sum_groups(l, c - 1)
        sum_groups(l, chunks - 1)
        rs2[l, zn - 1] = part[l, zn - 1]

    def make_factor(l):
        wait(recv.at[RS2, l, 0], rs2.at[l, pl.ds(0, zn - 1)])
        total = jnp.sum(rs2[l], axis=0)
        first = pl.multiple_of(core * hr + lax.div(j, bn) * 8, 8)
        lane = pl.multiple_of(lax.rem(j, bn) * lw, lw)
        here = lax.broadcasted_iota(jnp.int32, (8, rn), 0) + first == lax.broadcasted_iota(jnp.int32, (8, rn), 1)
        scale = jnp.sum(jnp.where(here, rscale[l : l + 1, :], 0.0), axis=1, keepdims=True) * factor
        weighted = prec[l, pl.ds(first, 8), pl.ds(lane, lw)] * (
            scale * total - innov[l, pl.ds(first, 8), pl.ds(lane, lw)]
        )
        wz[l, zn - 1] = scale * weighted

        def one(p, _):
            remote(wz.at[l, zn - 1], wz.at[l, p], WZ, l, dev(j, xl, core, plane_back(p)), lax.div(p, cs)).start()
            return 0

        lax.fori_loop(0, zn - 1, one, 0)

    def spread_factor(l):
        for c in reversed(range(chunks)):
            low = c * cs
            others = cs - 1 if c == chunks - 1 else cs
            if others:
                wait(recv.at[WZ, l, c], wz.at[l, pl.ds(0, others)])
            to_groups(lambda jd: wz.at[l, pl.ds(low, cs)], wg.at[l, j, pl.ds(low, cs)], WG, l, c)
            wg[l, j, low : low + cs] = wz[l, low : low + cs]

    def start_adjoint(l):
        hs = zn // 2
        for h in (1, 0):
            low = h * hs
            for c in reversed(range(h * chunks // 2, (h + 1) * chunks // 2)):
                wait(recv.at[WG, l, c], wg.at[l, pl.ds(0, jn - 1), pl.ds(c * cs, cs)])
            for a in range(an):
                for b in range(bn):
                    lanes = slice(b * lw, (b + 1) * lw)
                    adj[low : low + hs, a, :, lanes] = (
                        wg[l, a * bn + b, low : low + hs] * erecv[l, low : low + hs, a, :, lanes]
                    )
            y = times_table(adj[low : low + hs].reshape(hs * hr, ny), col)
            for k in range(4):
                adjc[l, k, low : low + hs] = y[:, k * kc : (k + 1) * kc].reshape(hs, hr, kc)
            to_plane(
                lambda k, xd, cd: adjc.at[l, k, pl.ds(low, hs)], ax.at[l, xl, pl.ds(low, hs), core], AX, l, h
            )
            ax[l, xl, low : low + hs, core] = adjc[l, q, low : low + hs]

    def adjoint(l):
        hs = zn // 2
        for h in (1, 0):
            wait(recv.at[AX, l, h], adjc.at[l, pl.ds(0, 3), pl.ds(0, hs)])

        def place(p, _):
            nat[:, plane_of(p)] = ax[l, :, p]
            return 0

        lax.fori_loop(0, zn, place, 0)
        top, bottom = rows(l, nat[...].reshape(nx, kc))
        gout[l, 0] = top.reshape(zn, rn, kc)
        gout[l, 1] = bottom.reshape(zn, rn, kc)

    def finish(l):
        wait(recv.at[G, l, 0], grecv.at[l])
        x = jnp.concatenate([grecv[l, :, k].reshape(mn * rn, kc) for k in range(4)], axis=1)
        out[:, l] = ctrl[:, l] + times_table(x, icol).reshape(mn, rn, ny)

    loads[0].wait()
    loads[1].wait()
    columns(0)
    loads[2].wait()
    core_k = pl.multiple_of(core * kb, kb)
    piece = pl.multiple_of(j * px, px)
    specz[:, z] = spec[:, pl.ds(core_k, kb), pl.ds(piece, px)]
    pl.semaphore_wait(barrier, 4 * zn - 1 + jn - 1)

    def send_spec(t, _):
        remote(specz.at[:, z], specz.at[:, z], SPZ, 0, dev(j, xl, core, lax.rem(z + t, zn))).start()
        return 0

    lax.fori_loop(1, zn, send_spec, 0)
    send_control(0, 0, zn)
    loads[3].wait()
    widen(0)
    send_ensemble(0, 0, zn)
    for load in loads[5:]:
        load.start()
    loads[4].wait()
    columns(1)
    widen(1)
    for load in loads[5:]:
        load.wait()

    wait(recv.at[SPZ, 0, 0], specz.at[:, pl.ds(0, zn - 1)])
    to_groups(lambda jd: specz, specg.at[j], SPG, 0)
    specg[j] = specz[...]
    wait(recv.at[SPG, 0, 0], specg.at[pl.ds(0, jn - 1)])
    for l in range(2):
        for k in range(jn):
            spect[l, k * px : (k + 1) * px] = specg[k, l].reshape(kc, px).T

    start_alpha(0)
    make_alpha(0)
    sum_members(0)
    feed(0, 2)
    make_factor(0)
    feed(0, 3)
    spread_factor(0)
    feed(0, 4)
    start_alpha(1)
    start_adjoint(0)
    make_alpha(1)
    sum_members(1)
    adjoint(0)
    feed(1, 2)
    make_factor(1)
    feed(1, 3)
    spread_factor(1)
    feed(1, 4)
    start_adjoint(1)
    adjoint(1)
    send_gradient(1, 0, zn)
    finish(0)
    finish(1)

    wait(send.at[SPZ, 0], specz.at[:, pl.ds(0, zn - 1)])
    wait(send.at[SPG, 0], specg.at[pl.ds(0, jn - 1)])

    def sent(l, _):
        wait(send.at[GX, l], gx.at[l, pl.ds(0, 3)])
        wait(send.at[AX, l], adjc.at[l, pl.ds(0, 3)])
        wait(send.at[RS1, l], rs1.at[l, pl.ds(0, jn - 1)])
        wait(send.at[WG, l], wg.at[l, pl.ds(0, jn - 1)])
        wait(send.at[RS2, l], rs2.at[l, pl.ds(0, zn - 1)])
        wait(send.at[WZ, l], wz.at[l, pl.ds(0, zn - 1)])

        @pl.when(in_plane_set)
        def _():
            wait(send.at[C, l], crecv.at[l, 0])
            wait(send.at[C, l], crecv.at[l, 1, pl.ds(0, zn - 1)])
            wait(send.at[E, l], erecv.at[l, pl.ds(0, zn - 1)])
            wait(send.at[G, l], gout.at[l, 0])
            wait(send.at[G, l], gout.at[l, 1, pl.ds(0, zn - 1)])

        @pl.when(jnp.logical_not(in_plane_set))
        def _():
            wait(send.at[C, l], crecv.at[l])
            wait(send.at[E, l], erecv.at[l])
            wait(send.at[G, l], gout.at[l])

        return 0

    lax.fori_loop(0, 2, sent, 0)


def body(zn, jn, members_all, interpret_lanes, ensemble, control, spectrum, row_scale, precision, innovation):
    mn, _, rn, ny = control.shape
    nx = spectrum.shape[2]
    kb = spectrum.shape[1] // 2
    kc, hr, px = ny // 4, rn // 2, nx // jn
    lw = interpret_lanes
    an = hr // 8
    assert mn * 2 == zn and an * (ny // lw) == jn and kb * zn == kc
    h_col, h_row = hartley_matrix(ny), hartley_matrix(nx)
    k = np.arange(ny).reshape(2, zn, 2, kb).transpose(0, 2, 1, 3).reshape(-1)
    col, icol = two_parts(h_col[:, k]), two_parts(h_col[k, :])
    even, odd = h_row[0::2, : nx // 2], h_row[1::2, : nx // 2]
    row = np.stack([two_parts(even), two_parts(odd), two_parts(odd.T)])
    f32 = jnp.float32
    vmem, anyspace = pl.BlockSpec(memory_space=pltpu.VMEM), pl.BlockSpec(memory_space=pl.ANY)
    return pl.pallas_call(
        functools.partial(kernel, zn, jn, 1.0 / math.sqrt(members_all - 1)),
        out_shape=jax.ShapeDtypeStruct(control.shape, f32),
        in_specs=[anyspace] * 9,
        out_specs=vmem,
        scratch_shapes=[
            pltpu.VMEM(control.shape, f32),
            pltpu.VMEM(ensemble.shape, ensemble.dtype),
            pltpu.VMEM(spectrum.shape, f32),
            pltpu.VMEM(row_scale.shape, f32),
            pltpu.VMEM(precision.shape, f32),
            pltpu.VMEM(innovation.shape, f32),
            pltpu.VMEM(col.shape, jnp.bfloat16),
            pltpu.VMEM(icol.shape, jnp.bfloat16),
            pltpu.VMEM(row.shape, jnp.bfloat16),
            pltpu.VMEM((2, mn, 4, rn, kc), f32),
            pltpu.VMEM((2, 2, zn, rn, kc), f32),
            pltpu.VMEM((2, mn, 2, an, 8, ny), f32),
            pltpu.VMEM((2, zn, an, 8, ny), f32),
            pltpu.VMEM((2, zn, kb, px), f32),
            pltpu.VMEM((jn, 2, zn, kb, px), f32),
            pltpu.VMEM((2, nx, kc), f32),
            pltpu.VMEM((2, 2, zn, 2, hr, kc), f32),
            pltpu.VMEM((2, 4, zn, hr, kc), f32),
            pltpu.VMEM((2, zn, an, 8, ny), f32),
            pltpu.VMEM((2, jn, zn, 8, lw), f32),
            pltpu.VMEM((2, jn, zn, 8, lw), f32),
            pltpu.VMEM((2, zn, 8, lw), f32),
            pltpu.VMEM((2, zn, 8, lw), f32),
            pltpu.VMEM((2, zn, 8, lw), f32),
            pltpu.VMEM((2, jn, zn, 8, lw), f32),
            pltpu.VMEM((zn, an, 8, ny), f32),
            pltpu.VMEM((2, 4, zn, hr, kc), f32),
            pltpu.VMEM((2, 2, zn, 2, hr, kc), f32),
            pltpu.VMEM((2, zn, 2, hr, kc), f32),
            pltpu.VMEM((2, 2, zn, rn, kc), f32),
            pltpu.VMEM((2, mn, 4, rn, kc), f32),
            pltpu.SemaphoreType.DMA((11, 2)),
            pltpu.SemaphoreType.DMA((11, 2, 4)),
            pltpu.SemaphoreType.DMA((10,)),
        ],
        compiler_params=pltpu.CompilerParams(
            collective_id=0, has_side_effects=True, vmem_limit_bytes=63 * 1024 * 1024
        ),
        name="gradient",
    )(control, ensemble, spectrum, row_scale, precision, innovation, jnp.asarray(col), jnp.asarray(icol), jnp.asarray(row))


def solution(mesh, lanes=128):
    zn, jn = mesh.shape["space"] // 2, mesh.shape["ens"] // 2
    in_specs = (
        P("ens", None, "space", None),
        P("ens", None, "space", None),
        P(None, "space", None),
        P(None, "space"),
        P(None, "space", None),
        P(None, "space", None),
    )
    out_specs = P("ens", None, "space", None)

    def whole(ensemble, *rest):
        step = functools.partial(body, zn, jn, ensemble.shape[0], lanes)
        return jax.shard_map(step, mesh=mesh, in_specs=in_specs, out_specs=out_specs, check_vma=False)(ensemble, *rest)

    return whole
```

```python
import functools
import math

import jax
import jax.numpy as jnp
import ml_dtypes
import numpy as np
from jax import lax
from jax.experimental import pallas as pl
from jax.experimental.pallas import tpu as pltpu
from jax.sharding import PartitionSpec as P

MESH = pl.DeviceIdType.MESH
SPZ, SPG, C, E, GX, RS1, RS2, WZ, WG, AX, G = range(11)
FEED = ((2, 3, 13, 32, 32), (0, 0, 0, 16, 16))


def hartley_matrix(n):
    index = np.arange(n, dtype=np.int64)
    angle = (index[:, None] * index[None, :] % n) * (2.0 * math.pi / n)
    return (np.cos(angle) + np.sin(angle)) / math.sqrt(n)


def two_parts(table):
    high = table.astype(ml_dtypes.bfloat16)
    low = (table - high.astype(np.float64)).astype(ml_dtypes.bfloat16)
    return np.stack([high, low])


def dot(a, b):
    return jnp.dot(a, b, preferred_element_type=jnp.float32)


def parts_of(x):
    high = x.astype(jnp.bfloat16)
    return high, (x - high.astype(jnp.float32)).astype(jnp.bfloat16)


def times_table(x, table):
    high, low = parts_of(x)
    return dot(high, table[0]) + dot(low, table[0]) + dot(high, table[1])


def table_times(table, k, y):
    high, low = parts_of(y)
    width = y.shape[1]
    both = dot(table[k, 0], jnp.concatenate([high, low], axis=1))
    return both[:, :width] + both[:, width:] + dot(table[k, 1], high)


def kernel(
    zn, jn, factor,
    ctrl_hbm, ens_hbm, spec_hbm, rscale_hbm, prec_hbm, innov_hbm, col_hbm, icol_hbm, row_hbm,
    out,
    ctrl, ens, spec, rscale, prec, innov, col, icol, row,
    cst, crecv, e32, erecv, specz, specg, spect, field, gx, alpha, prod, rs1, part, rs2, wz, wg, adj, adjc, ax, nat, gout,
    grecv, send, recv, local_sem,
):
    mn, _, rn, ny = ctrl.shape
    nx = spec.shape[2]
    kb = spec.shape[1] // 2
    kc = ny // 4
    hr = rn // 2
    half = nx // 2
    lw = prod.shape[4]
    bn = ny // lw
    an = jn // bn
    px = nx // jn
    chunks = min(2, zn)
    cs = zn // chunks
    ei, si = lax.axis_index("ens"), lax.axis_index("space")
    j, core = lax.div(ei, 2), lax.rem(ei, 2)
    xl, z = lax.div(si, zn), lax.rem(si, zn)
    q = xl * 2 + core
    owner_core = lax.div(z, mn)
    member = lax.rem(z, mn)
    in_plane_set = owner_core == core

    def dev(j_, xl_, core_, z_):
        return (j_ * 2 + core_, xl_ * zn + z_)

    def remote(src, dst, phase, l, device, c=0):
        return pltpu.make_async_remote_copy(
            src_ref=src, dst_ref=dst, send_sem=send.at[phase, l], recv_sem=recv.at[phase, l, c],
            device_id=device, device_id_type=MESH,
        )

    def wait(sem, ref):
        pltpu.make_async_copy(ref, ref, sem).wait()

    def offset(p):
        far = lax.div(zn - p, 2)
        return jnp.where(lax.rem(p, 2) == 1, far, -far)

    def plane_of(p):
        return lax.rem(z + offset(p) + zn, zn)

    def plane_back(p):
        return lax.rem(z - offset(p) + zn, zn)

    loads = [
        pltpu.make_async_copy(src, dst, local_sem.at[i])
        for i, (src, dst) in enumerate(
            [
                (ctrl_hbm.at[:, 0], ctrl.at[:, 0]), (col_hbm, col), (spec_hbm, spec), (ens_hbm, ens),
                (ctrl_hbm.at[:, 1], ctrl.at[:, 1]), (row_hbm, row), (icol_hbm, icol), (rscale_hbm, rscale),
                (prec_hbm, prec), (innov_hbm, innov),
            ]
        )
    ]
    barrier = pltpu.get_barrier_semaphore()
    mine = q * zn + z

    def greet_group(t, _):
        other = lax.rem(mine + t, 4 * zn)
        oq, oz = lax.div(other, zn), lax.rem(other, zn)
        pl.semaphore_signal(barrier, inc=1, device_id=dev(j, lax.div(oq, 2), lax.rem(oq, 2), oz), device_id_type=MESH)
        return 0

    lax.fori_loop(1, 4 * zn, greet_group, 0)

    def greet_others(t, _):
        pl.semaphore_signal(barrier, inc=1, device_id=dev(lax.rem(j + t, jn), xl, core, z), device_id_type=MESH)
        return 0

    lax.fori_loop(1, jn, greet_others, 0)
    for load in loads[:5]:
        load.start()

    def columns(l):
        y = times_table(ctrl[:, l].reshape(mn * rn, ny), col)
        for k in range(4):
            cst[l, :, k] = y[:, k * kc : (k + 1) * kc].reshape(mn, rn, kc)

    def widen(l):
        for m in range(mn):
            e32[l, m] = ens[m, l].astype(jnp.float32).reshape(2, an, 8, ny)

    def either(same, src, dst, phase, l, device, c=0):
        @pl.when(same)
        def _():
            pltpu.make_async_copy(src, dst, recv.at[phase, l, c]).start()

        @pl.when(jnp.logical_not(same))
        def _():
            remote(src, dst, phase, l, device, c).start()

    def send_control(l, low, high):
        def one(p, _):
            zd = plane_back(p)

            @pl.when(lax.div(zd, mn) == core)
            def _():
                for k in range(4):
                    remote(cst.at[l, lax.rem(zd, mn), k], crecv.at[l, xl, z], C, l, dev(j, k // 2, k % 2, zd)).start()

            return 0

        lax.fori_loop(low, min(high, zn - 1), one, 0)
        if low < high == zn:

            @pl.when(in_plane_set)
            def _():
                for k in range(4):
                    either(q == k, cst.at[l, member, k], crecv.at[l, xl, z], C, l, dev(j, k // 2, k % 2, z))

    def send_ensemble(l, low, high):
        def one(p, _):
            zd = plane_back(p)

            @pl.when(lax.div(zd, mn) == core)
            def _():
                for k in range(2):
                    remote(
                        e32.at[l, lax.rem(zd, mn), k], erecv.at[l, p], E, l, dev(j, xl, k, zd), lax.div(p, cs)
                    ).start()

            return 0

        lax.fori_loop(low, min(high, zn - 1), one, 0)
        if low < high == zn:

            @pl.when(in_plane_set)
            def _():
                for k in range(2):
                    either(core == k, e32.at[l, member, k], erecv.at[l, zn - 1], E, l, dev(j, xl, k, z), chunks - 1)

    def send_gradient(l, low, high):
        def one(p, _):
            zd = plane_back(p)
            for k in range(2):
                remote(gout.at[l, k, zd], grecv.at[l, member, q], G, l, dev(j, k, owner_core, zd)).start()
            return 0

        lax.fori_loop(low, min(high, zn - 1), one, 0)
        if low < high == zn:
            for k in range(2):
                either(
                    in_plane_set & (xl == k), gout.at[l, k, z], grecv.at[l, member, q], G, l, dev(j, k, owner_core, z)
                )

    def to_groups(src_of, dst, phase, l, c=0):
        def one(t, _):
            jd = lax.rem(j + t, jn)
            remote(src_of(jd), dst, phase, l, dev(jd, xl, core, z), c).start()
            return 0

        lax.fori_loop(1, jn, one, 0)

    def to_plane(src_of, dst, phase, l, c=0):
        def one(t, _):
            k = lax.rem(q + t, 4)
            xd, cd = lax.div(k, 2), lax.rem(k, 2)
            remote(src_of(k, xd, cd), dst, phase, l, dev(j, xd, cd, z), c).start()
            return 0

        lax.fori_loop(1, 4, one, 0)

    def rows(l, y):
        even = table_times(row, 0, y[:half] + y[half:]) * spect[l, pl.ds(0, half, 2), :]
        odd = table_times(row, 1, y[:half] - y[half:]) * spect[l, pl.ds(1, half, 2), :]
        a = table_times(row, 0, even)
        b = table_times(row, 2, odd)
        return a + b, a - b

    def start_alpha(l):
        wait(recv.at[C, l, 0], crecv.at[l])
        top, bottom = rows(l, crecv[l].reshape(nx, kc))
        field[l, 0] = top.reshape(zn, 2, hr, kc)
        field[l, 1] = bottom.reshape(zn, 2, hr, kc)
        to_plane(lambda k, xd, cd: field.at[l, xd, :, cd], gx.at[l, q], GX, l)
        gx[l, q] = field[l, xl, :, core]

    def make_alpha(l):
        wait(recv.at[GX, l, 0], gx.at[l, pl.ds(0, 3)])
        x = jnp.concatenate([gx[l, k].reshape(zn * hr, kc) for k in range(4)], axis=1)
        alpha[l] = times_table(x, icol).reshape(zn, an, 8, ny)

    def feed(l, point):
        low = FEED[l][point - 1] * zn // 16 if point else 0
        high = FEED[l][point] * zn // 16
        if l == 0:
            send_control(1, min(low, zn), min(high, zn))
            send_ensemble(1, max(low - zn, 0), max(high - zn, 0))
        else:
            send_gradient(0, low, high)

    def sum_groups(l, c):
        low, high = c * cs, (c + 1) * cs
        wait(recv.at[RS1, l, c], rs1.at[l, pl.ds(0, jn - 1), pl.ds(low, cs)])
        part[l, low:high] = jnp.sum(rs1[l, :, low:high], axis=0)

        def one(p, _):
            remote(part.at[l, p], rs2.at[l, p], RS2, l, dev(j, xl, core, plane_of(p))).start()
            return 0

        lax.fori_loop(low, min(high, zn - 1), one, 0)

    def sum_members(l):
        for c in range(chunks):
            low = c * cs
            if c >= chunks - 2:
                feed(l, c - (chunks - 2))
            wait(recv.at[E, l, c], erecv.at[l, pl.ds(low, cs)])

            def multiply(p, _):
                here = plane_of(p)
                for a in range(an):
                    for b in range(bn):
                        lanes = slice(b * lw, (b + 1) * lw)
                        prod[l, a * bn + b, p] = alpha[l, here, a, :, lanes] * erecv[l, p, a, :, lanes]
                return 0

            lax.fori_loop(low, low + cs, multiply, 0)
            to_groups(lambda jd: prod.at[l, jd, pl.ds(low, cs)], rs1.at[l, j, pl.ds(low, cs)], RS1, l, c)
            rs1[l, j, low : low + cs] = prod[l, j, low : low + cs]
            if c > 0:
                sum_groups(l, c - 1)
        sum_groups(l, chunks - 1)
        rs2[l, zn - 1] = part[l, zn - 1]

    def make_factor(l):
        wait(recv.at[RS2, l, 0], rs2.at[l, pl.ds(0, zn - 1)])
        total = jnp.sum(rs2[l], axis=0)
        first = pl.multiple_of(core * hr + lax.div(j, bn) * 8, 8)
        lane = pl.multiple_of(lax.rem(j, bn) * lw, lw)
        here = lax.broadcasted_iota(jnp.int32, (8, rn), 0) + first == lax.broadcasted_iota(jnp.int32, (8, rn), 1)
        scale = jnp.sum(jnp.where(here, rscale[l : l + 1, :], 0.0), axis=1, keepdims=True) * factor
        weighted = prec[l, pl.ds(first, 8), pl.ds(lane, lw)] * (
            scale * total - innov[l, pl.ds(first, 8), pl.ds(lane, lw)]
        )
        wz[l, zn - 1] = scale * weighted

        def one(p, _):
            remote(wz.at[l, zn - 1], wz.at[l, p], WZ, l, dev(j, xl, core, plane_back(p)), lax.div(p, cs)).start()
            return 0

        lax.fori_loop(0, zn - 1, one, 0)

    def spread_factor(l):
        for c in reversed(range(chunks)):
            low = c * cs
            others = cs - 1 if c == chunks - 1 else cs
            if others:
                wait(recv.at[WZ, l, c], wz.at[l, pl.ds(0, others)])
            to_groups(lambda jd: wz.at[l, pl.ds(low, cs)], wg.at[l, j, pl.ds(low, cs)], WG, l, c)
            wg[l, j, low : low + cs] = wz[l, low : low + cs]

    def start_adjoint(l):
        hs = zn // 2
        for h in (1, 0):
            low = h * hs
            for c in reversed(range(h * chunks // 2, (h + 1) * chunks // 2)):
                wait(recv.at[WG, l, c], wg.at[l, pl.ds(0, jn - 1), pl.ds(c * cs, cs)])
            for a in range(an):
                for b in range(bn):
                    lanes = slice(b * lw, (b + 1) * lw)
                    adj[low : low + hs, a, :, lanes] = (
                        wg[l, a * bn + b, low : low + hs] * erecv[l, low : low + hs, a, :, lanes]
                    )
            y = times_table(adj[low : low + hs].reshape(hs * hr, ny), col)
            for k in range(4):
                adjc[l, k, low : low + hs] = y[:, k * kc : (k + 1) * kc].reshape(hs, hr, kc)
            to_plane(
                lambda k, xd, cd: adjc.at[l, k, pl.ds(low, hs)], ax.at[l, xl, pl.ds(low, hs), core], AX, l, h
            )
            ax[l, xl, low : low + hs, core] = adjc[l, q, low : low + hs]

    def adjoint(l):
        hs = zn // 2
        for h in (1, 0):
            wait(recv.at[AX, l, h], adjc.at[l, pl.ds(0, 3), pl.ds(0, hs)])

        def place(p, _):
            nat[:, plane_of(p)] = ax[l, :, p]
            return 0

        lax.fori_loop(0, zn, place, 0)
        top, bottom = rows(l, nat[...].reshape(nx, kc))
        gout[l, 0] = top.reshape(zn, rn, kc)
        gout[l, 1] = bottom.reshape(zn, rn, kc)

    def finish(l):
        wait(recv.at[G, l, 0], grecv.at[l])
        x = jnp.concatenate([grecv[l, :, k].reshape(mn * rn, kc) for k in range(4)], axis=1)
        out[:, l] = ctrl[:, l] + times_table(x, icol).reshape(mn, rn, ny)

    loads[0].wait()
    loads[1].wait()
    columns(0)
    loads[2].wait()
    core_k = pl.multiple_of(core * kb, kb)
    piece = pl.multiple_of(j * px, px)
    specz[:, z] = spec[:, pl.ds(core_k, kb), pl.ds(piece, px)]
    pl.semaphore_wait(barrier, 4 * zn - 1 + jn - 1)

    def send_spec(t, _):
        remote(specz.at[:, z], specz.at[:, z], SPZ, 0, dev(j, xl, core, lax.rem(z + t, zn))).start()
        return 0

    lax.fori_loop(1, zn, send_spec, 0)
    send_control(0, 0, zn)
    loads[3].wait()
    widen(0)
    send_ensemble(0, 0, zn)
    for load in loads[5:]:
        load.start()
    loads[4].wait()
    columns(1)
    widen(1)
    for load in loads[5:]:
        load.wait()

    wait(recv.at[SPZ, 0, 0], specz.at[:, pl.ds(0, zn - 1)])
    to_groups(lambda jd: specz, specg.at[j], SPG, 0)
    specg[j] = specz[...]
    wait(recv.at[SPG, 0, 0], specg.at[pl.ds(0, jn - 1)])
    for l in range(2):
        for k in range(jn):
            spect[l, k * px : (k + 1) * px] = specg[k, l].reshape(kc, px).T

    start_alpha(0)
    make_alpha(0)
    sum_members(0)
    feed(0, 2)
    make_factor(0)
    feed(0, 3)
    spread_factor(0)
    feed(0, 4)
    start_alpha(1)
    start_adjoint(0)
    make_alpha(1)
    sum_members(1)
    adjoint(0)
    feed(1, 2)
    make_factor(1)
    feed(1, 3)
    spread_factor(1)
    feed(1, 4)
    start_adjoint(1)
    adjoint(1)
    send_gradient(1, 0, zn)
    finish(0)
    finish(1)

    wait(send.at[SPZ, 0], specz.at[:, pl.ds(0, zn - 1)])
    wait(send.at[SPG, 0], specg.at[pl.ds(0, jn - 1)])

    def sent(l, _):
        wait(send.at[GX, l], gx.at[l, pl.ds(0, 3)])
        wait(send.at[AX, l], adjc.at[l, pl.ds(0, 3)])
        wait(send.at[RS1, l], rs1.at[l, pl.ds(0, jn - 1)])
        wait(send.at[WG, l], wg.at[l, pl.ds(0, jn - 1)])
        wait(send.at[RS2, l], rs2.at[l, pl.ds(0, zn - 1)])
        wait(send.at[WZ, l], wz.at[l, pl.ds(0, zn - 1)])

        @pl.when(in_plane_set)
        def _():
            wait(send.at[C, l], crecv.at[l, 0])
            wait(send.at[C, l], crecv.at[l, 1, pl.ds(0, zn - 1)])
            wait(send.at[E, l], erecv.at[l, pl.ds(0, zn - 1)])
            wait(send.at[G, l], gout.at[l, 0])
            wait(send.at[G, l], gout.at[l, 1, pl.ds(0, zn - 1)])

        @pl.when(jnp.logical_not(in_plane_set))
        def _():
            wait(send.at[C, l], crecv.at[l])
            wait(send.at[E, l], erecv.at[l])
            wait(send.at[G, l], gout.at[l])

        return 0

    lax.fori_loop(0, 2, sent, 0)


def body(zn, jn, members_all, interpret_lanes, ensemble, control, spectrum, row_scale, precision, innovation):
    mn, _, rn, ny = control.shape
    nx = spectrum.shape[2]
    kb = spectrum.shape[1] // 2
    kc, hr, px = ny // 4, rn // 2, nx // jn
    lw = interpret_lanes
    an = hr // 8
    assert mn * 2 == zn and an * (ny // lw) == jn and kb * zn == kc
    h_col, h_row = hartley_matrix(ny), hartley_matrix(nx)
    k = np.arange(ny).reshape(2, zn, 2, kb).transpose(0, 2, 1, 3).reshape(-1)
    col, icol = two_parts(h_col[:, k]), two_parts(h_col[k, :])
    even, odd = h_row[0::2, : nx // 2], h_row[1::2, : nx // 2]
    row = np.stack([two_parts(even), two_parts(odd), two_parts(odd.T)])
    f32 = jnp.float32
    vmem, anyspace = pl.BlockSpec(memory_space=pltpu.VMEM), pl.BlockSpec(memory_space=pl.ANY)
    return pl.pallas_call(
        functools.partial(kernel, zn, jn, 1.0 / math.sqrt(members_all - 1)),
        out_shape=jax.ShapeDtypeStruct(control.shape, f32),
        in_specs=[anyspace] * 9,
        out_specs=vmem,
        scratch_shapes=[
            pltpu.VMEM(control.shape, f32),
            pltpu.VMEM(ensemble.shape, ensemble.dtype),
            pltpu.VMEM(spectrum.shape, f32),
            pltpu.VMEM(row_scale.shape, f32),
            pltpu.VMEM(precision.shape, f32),
            pltpu.VMEM(innovation.shape, f32),
            pltpu.VMEM(col.shape, jnp.bfloat16),
            pltpu.VMEM(icol.shape, jnp.bfloat16),
            pltpu.VMEM(row.shape, jnp.bfloat16),
            pltpu.VMEM((2, mn, 4, rn, kc), f32),
            pltpu.VMEM((2, 2, zn, rn, kc), f32),
            pltpu.VMEM((2, mn, 2, an, 8, ny), f32),
            pltpu.VMEM((2, zn, an, 8, ny), f32),
            pltpu.VMEM((2, zn, kb, px), f32),
            pltpu.VMEM((jn, 2, zn, kb, px), f32),
            pltpu.VMEM((2, nx, kc), f32),
            pltpu.VMEM((2, 2, zn, 2, hr, kc), f32),
            pltpu.VMEM((2, 4, zn, hr, kc), f32),
            pltpu.VMEM((2, zn, an, 8, ny), f32),
            pltpu.VMEM((2, jn, zn, 8, lw), f32),
            pltpu.VMEM((2, jn, zn, 8, lw), f32),
            pltpu.VMEM((2, zn, 8, lw), f32),
            pltpu.VMEM((2, zn, 8, lw), f32),
            pltpu.VMEM((2, zn, 8, lw), f32),
            pltpu.VMEM((2, jn, zn, 8, lw), f32),
            pltpu.VMEM((zn, an, 8, ny), f32),
            pltpu.VMEM((2, 4, zn, hr, kc), f32),
            pltpu.VMEM((2, 2, zn, 2, hr, kc), f32),
            pltpu.VMEM((2, zn, 2, hr, kc), f32),
            pltpu.VMEM((2, 2, zn, rn, kc), f32),
            pltpu.VMEM((2, mn, 4, rn, kc), f32),
            pltpu.SemaphoreType.DMA((11, 2)),
            pltpu.SemaphoreType.DMA((11, 2, 4)),
            pltpu.SemaphoreType.DMA((10,)),
        ],
        compiler_params=pltpu.CompilerParams(
            collective_id=0, has_side_effects=True, vmem_limit_bytes=63 * 1024 * 1024
        ),
        name="gradient",
    )(control, ensemble, spectrum, row_scale, precision, innovation, jnp.asarray(col), jnp.asarray(icol), jnp.asarray(row))


def solution(mesh, lanes=128):
    zn, jn = mesh.shape["space"] // 2, mesh.shape["ens"] // 2
    in_specs = (
        P("ens", None, "space", None),
        P("ens", None, "space", None),
        P(None, "space", None),
        P(None, "space"),
        P(None, "space", None),
        P(None, "space", None),
    )
    out_specs = P("ens", None, "space", None)

    def whole(ensemble, *rest):
        step = functools.partial(body, zn, jn, ensemble.shape[0], lanes)
        return jax.shard_map(step, mesh=mesh, in_specs=in_specs, out_specs=out_specs, check_vma=False)(ensemble, *rest)

    return whole
```
